32 devices in a mesh: dp: 2 (over core), mp: 4 (over y, x), hidden: 4 (over z).
Axes of the slice: x: 2, y: 2, z: 4, core: 2. Of those that a mesh axis runs over, the one named last changes fastest.
Arguments:
- tokens: bfloat16 [1024, 8192], P('dp', 'mp'), may hold values from -6 to 6
- out_grad: bfloat16 [1024, 8192], P('dp', 'mp'), may hold values from -6 to 6
- gate_weight: bfloat16 [8192, 14336], P('mp', 'hidden'), may hold values from -0.0625 to 0.0625
- up_weight: bfloat16 [8192, 14336], P('mp', 'hidden'), may hold values from -0.0625 to 0.0625
- down_weight: bfloat16 [14336, 8192], P('hidden', 'mp'), may hold values from -0.046875 to 0.046875
- gate_keep: int32 [64, 112], P('mp', 'hidden'), may hold values from 0 to 1, as said below
- up_keep: int32 [64, 112], P('mp', 'hidden'), may hold values from 0 to 1, as said below
- down_keep: int32 [112, 64], P('hidden', 'mp'), may hold values from 0 to 1, as said below
- hidden_order: int32 [112], replicated, may hold values from 0 to 111, as said below
Outputs:
- gate_grad: bfloat16 [8192, 14336], P('mp', 'hidden')
- up_grad: bfloat16 [8192, 14336], P('mp', 'hidden')
- down_grad: bfloat16 [14336, 8192], P('hidden', 'mp')
The draws below stay inside these ranges and needn't reach their ends.
Inputs may be any that keep to these rules, and one draw needn't show every extreme that they name: `gate_keep`: each block is kept or not; the share kept differs from one hidden block to another. `up_keep`: each block is kept or not; the share kept differs from one hidden block to another. `down_keep`: each block is kept or not; the share kept differs from one hidden block to another. `hidden_order`: A permutation of the hidden blocks. Of the 28 entries in each aligned group of 28 (the row blocks of down_weight on one index of hidden), at most 7 name hidden blocks in any one aligned group of 28 hidden blocks (the gate columns of one index of hidden), and some group reaches 7.
All inputs are finite; a program needn't handle non-finite values.
Results may differ from the reference program's by a relative error of at most 0.0067.
Values may be sent and summed in bfloat16 or wider, within the bound.
A program may use at most 320 MiB of HBM per device.

```python
import jax
import jax.numpy as jnp

D = 8192
FF = 14336
BLK = 128
TOK_DEV = 512
TOKENS = 1024
BLK_DEV = 28
CAP = 7
N_DP = 2
N_HIDDEN = 4


def keep_blocks(key, rows, cols):
    first, second = jax.random.split(key)
    level = jax.random.randint(first, (1, cols), 5, 66)
    roll = jax.random.randint(second, (rows, cols), 0, 100)
    return (roll < level).astype(jnp.int32)


def draw_gate_keep(key, part):
    key = jax.random.fold_in(key, 11)
    return keep_blocks(key, D // BLK, FF // BLK)


def draw_up_keep(key, part):
    key = jax.random.fold_in(key, 12)
    return keep_blocks(key, D // BLK, FF // BLK)


def draw_down_keep(key, part):
    key = jax.random.fold_in(key, 13)
    return keep_blocks(key, D // BLK, FF // BLK).T


def draw_hidden_order(key, part):
    key = jax.random.fold_in(key, 14)
    first, second, third, fourth = jax.random.split(key, 4)
    ways = N_HIDDEN
    count = BLK_DEV
    pick = jax.random.permutation(first, ways * CAP)[:count]
    offset = (pick % ways).astype(jnp.int32)
    relabel = jax.random.permutation(second, ways).astype(jnp.int32)
    position = jax.random.permutation(third, ways).astype(jnp.int32)
    dest = jnp.arange(ways, dtype=jnp.int32)
    source = relabel[(position[dest][:, None] + offset[None, :]) % ways]
    scores = jax.random.randint(fourth, (ways, count), 0, 1 << 20) * count + jnp.arange(count, dtype=jnp.int32)[None, :]
    local_order = jnp.argsort(scores, axis=1).astype(jnp.int32)
    column = jnp.broadcast_to(jnp.arange(count, dtype=jnp.int32)[None, :], (ways, count))
    local = local_order[source, column]
    return (source * count + local).reshape(-1).astype(jnp.int32)


def block_levels(key, dims, cuts, least, top_value):
    loudness = 1.0
    for dim, shards_of in cuts:
        steps = jax.random.uniform(jax.random.fold_in(jax.random.fold_in(key, 6), dim), (shards_of,), jnp.float32, least / len(cuts), top_value / len(cuts))
        loudness = loudness * jnp.repeat(jnp.exp(steps), dims[dim] // shards_of).reshape((-1,) + (1,) * (len(dims) - 1 - dim))
    return loudness


def bell_draw(own_key, shape, scale, most, shards=(), kind=jnp.bfloat16):
    loudness = block_levels(own_key, shape, shards, -0.22, 0.18) if shards else 1.0
    drawn = jax.random.normal(own_key, shape, jnp.float32) * scale * loudness
    return jnp.minimum(jnp.maximum(drawn, -most), most).astype(kind)


def setup_inputs(seed: int = 0) -> dict:
    keys = jax.random.split(jax.random.key(seed), 10)
    tokens = bell_draw(keys[0], (TOKENS, D), 1.0, 6.0, ((0, 2), (1, 4)))
    out_grad = bell_draw(keys[1], (TOKENS, D), 1.0, 6.0, ((0, 2), (1, 4)))
    gate_weight = bell_draw(keys[2], (D, FF), D ** -0.5, 0.0625, ((0, 4), (1, 4)))
    up_weight = bell_draw(keys[3], (D, FF), D ** -0.5, 0.0625, ((0, 4), (1, 4)))
    down_weight = bell_draw(keys[4], (FF, D), FF ** -0.5, 0.046875, ((0, 4), (1, 4)))
    gate_keep = draw_gate_keep(jax.random.fold_in(keys[9], 71), 0)
    up_keep = draw_up_keep(jax.random.fold_in(keys[9], 71), 0)
    down_keep = draw_down_keep(jax.random.fold_in(keys[9], 71), 0)
    hidden_order = draw_hidden_order(jax.random.fold_in(keys[9], 71), 0)
    return {"tokens": tokens, "out_grad": out_grad, "gate_weight": gate_weight, "up_weight": up_weight, "down_weight": down_weight, "gate_keep": gate_keep, "up_keep": up_keep, "down_keep": down_keep, "hidden_order": hidden_order}


def spread(keep):
    return jnp.repeat(jnp.repeat(keep.astype(jnp.bfloat16), BLK, 0), BLK, 1)


def reference(tokens, out_grad, gate_weight, up_weight, down_weight, gate_keep, up_keep, down_keep, hidden_order):
    gate_masked = gate_weight * spread(gate_keep)
    up_masked = up_weight * spread(up_keep)
    down_stored = down_weight * spread(down_keep)
    blocks_all = FF // BLK
    inverse = jnp.argsort(hidden_order).astype(jnp.int32)
    down_masked = down_stored.reshape(blocks_all, BLK, D)[inverse].reshape(FF, D)
    gate = jnp.dot(tokens, gate_masked, preferred_element_type=jnp.float32)
    up = jnp.dot(tokens, up_masked, preferred_element_type=jnp.float32)
    sig = jax.nn.sigmoid(gate)
    act = gate * sig
    hidden_act = (act * up).astype(jnp.bfloat16)
    hidden_grad = jnp.dot(out_grad, down_masked.T, preferred_element_type=jnp.float32).astype(jnp.bfloat16)
    gate_delta = (hidden_grad * up * (sig * (1.0 + gate * (1.0 - sig)))).astype(jnp.bfloat16)
    up_delta = (hidden_grad * act).astype(jnp.bfloat16)
    gate_mask = spread(gate_keep)
    up_mask = spread(up_keep)
    down_mask = spread(down_keep)
    gate_total = jnp.zeros((D, FF), jnp.float32)
    up_total = jnp.zeros((D, FF), jnp.float32)
    down_total = jnp.zeros((FF, D), jnp.float32)
    for group in range(N_DP):
        lo = group * TOK_DEV
        hi = lo + TOK_DEV
        tok_rows = tokens[lo:hi]
        gate_term = (jnp.dot(tok_rows.T, gate_delta[lo:hi], preferred_element_type=jnp.float32) * gate_mask).astype(jnp.bfloat16)
        up_term = (jnp.dot(tok_rows.T, up_delta[lo:hi], preferred_element_type=jnp.float32) * up_mask).astype(jnp.bfloat16)
        down_nat = jnp.dot(hidden_act[lo:hi].T, out_grad[lo:hi], preferred_element_type=jnp.float32)
        down_sto = down_nat.reshape(blocks_all, BLK, D)[hidden_order].reshape(FF, D)
        down_term = (down_sto * down_mask).astype(jnp.bfloat16)
        gate_total = gate_total + gate_term.astype(jnp.float32)
        up_total = up_total + up_term.astype(jnp.float32)
        down_total = down_total + down_term.astype(jnp.float32)
    return gate_total.astype(jnp.bfloat16), up_total.astype(jnp.bfloat16), down_total.astype(jnp.bfloat16)
```

```python
import functools

import jax
import jax.numpy as jnp
from jax import lax
from jax.experimental import pallas as pl
from jax.experimental.pallas import tpu as pltpu
from jax.sharding import PartitionSpec as P

BLK = 128
F32 = jnp.float32
BF16 = jnp.bfloat16
NN = (((1,), (0,)), ((), ()))
NT = (((1,), (1,)), ((), ()))
TN = (((0,), (0,)), ((), ()))
VMEM_LIMIT = 48 * 1024 * 1024


def tile_blocks(blocks):
    return max(t for t in (1, 2, 4) if blocks % t == 0)


def params():
    return pltpu.CompilerParams(vmem_limit_bytes=VMEM_LIMIT)


def cost(rows, inner, cols, nbytes):
    return pl.CostEstimate(flops=2 * rows * inner * cols, bytes_accessed=nbytes, transcendentals=0)


def masked_into(dst, src, keep, row0, col0):
    rows, cols = src.shape
    for i in range(rows // BLK):
        for j in range(cols // BLK):
            at = (slice(i * BLK, (i + 1) * BLK), slice(j * BLK, (j + 1) * BLK))
            block = src[at]
            dst[at] = jnp.where(keep[row0 + i, col0 + j] != 0, block, jnp.zeros_like(block))


def columns_kernel(tb, keep, x, w, out, held):
    masked_into(held, w, keep, 0, pl.program_id(0) * tb)
    out[...] = lax.dot_general(x[...], held[...], NN, preferred_element_type=F32).astype(BF16)


def rows_kernel(tb, keep, x, w, out, held):
    masked_into(held, w, keep, pl.program_id(0) * tb, 0)
    out[...] = lax.dot_general(x[...], held[...], NT, preferred_element_type=F32).astype(BF16)


def times_columns(x, w, keep):
    rows, depth = x.shape
    cols = w.shape[1]
    tb = tile_blocks(cols // BLK)
    tn = tb * BLK
    return pl.pallas_call(
        functools.partial(columns_kernel, tb),
        grid=(cols // tn,),
        out_shape=jax.ShapeDtypeStruct((rows, cols), BF16),
        in_specs=[
            pl.BlockSpec(memory_space=pltpu.SMEM),
            pl.BlockSpec((rows, depth), lambda j: (0, 0)),
            pl.BlockSpec((depth, tn), lambda j: (0, j)),
        ],
        out_specs=pl.BlockSpec((rows, tn), lambda j: (0, j)),
        scratch_shapes=[pltpu.VMEM((depth, tn), BF16)],
        compiler_params=params(),
        cost_estimate=cost(rows, depth, cols, 2 * depth * cols + 2 * rows * cols),
    )(keep, x, w)


def times_rows(x, w, keep):
    rows, depth = x.shape
    cols = w.shape[0]
    tb = tile_blocks(cols // BLK)
    tn = tb * BLK
    return pl.pallas_call(
        functools.partial(rows_kernel, tb),
        grid=(cols // tn,),
        out_shape=jax.ShapeDtypeStruct((rows, cols), BF16),
        in_specs=[
            pl.BlockSpec(memory_space=pltpu.SMEM),
            pl.BlockSpec((rows, depth), lambda j: (0, 0)),
            pl.BlockSpec((tn, depth), lambda j: (j, 0)),
        ],
        out_specs=pl.BlockSpec((rows, tn), lambda j: (0, j)),
        scratch_shapes=[pltpu.VMEM((tn, depth), BF16)],
        compiler_params=params(),
        cost_estimate=cost(rows, depth, cols, 2 * depth * cols + 2 * rows * cols),
    )(keep, x, w)


def store_masked(out, value, keep, row0, col0, base):
    rows, cols = value.shape
    for i in range(rows // BLK):
        for j in range(cols // BLK):
            block = value[i * BLK : (i + 1) * BLK, j * BLK : (j + 1) * BLK]
            out[base + i * BLK : base + (i + 1) * BLK, j * BLK : (j + 1) * BLK] = jnp.where(
                keep[row0 + i, col0 + j] != 0, block, jnp.zeros_like(block)
            ).astype(BF16)


def in_grad_kernel(tb, strip, keep, xt, d0, d1, out):
    col0 = pl.program_id(0) * tb
    half = d0.shape[0]
    for base in range(0, xt.shape[0], strip):
        value = lax.dot_general(
            xt[base : base + strip, :half], d0[...], NN, preferred_element_type=F32
        ) + lax.dot_general(xt[base : base + strip, half:], d1[...], NN, preferred_element_type=F32)
        store_masked(out, value, keep, base // BLK, col0, base)


def in_grad(xt, d0, d1, keep):
    rows, depth = xt.shape
    half, cols = d0.shape
    tb = tile_blocks(cols // BLK)
    tn = tb * BLK
    return pl.pallas_call(
        functools.partial(in_grad_kernel, tb, min(512, rows)),
        grid=(cols // tn,),
        out_shape=jax.ShapeDtypeStruct((rows, cols), BF16),
        in_specs=[
            pl.BlockSpec(memory_space=pltpu.SMEM),
            pl.BlockSpec((rows, depth), lambda j: (0, 0)),
            pl.BlockSpec((half, tn), lambda j: (0, j)),
            pl.BlockSpec((half, tn), lambda j: (0, j)),
        ],
        out_specs=pl.BlockSpec((rows, tn), lambda j: (0, j)),
        compiler_params=params(),
        cost_estimate=cost(rows, depth, cols, 2 * depth * cols + 2 * rows * cols),
    )(keep, xt, d0, d1)


def out_grad_kernel(tb, keep, m0, m1, g0, g1, out):
    row0 = pl.program_id(0) * tb
    value = lax.dot_general(m0[...], g0[...], TN, preferred_element_type=F32) + lax.dot_general(
        m1[...], g1[...], TN, preferred_element_type=F32
    )
    store_masked(out, value, keep, row0, 0, 0)


def down_grad(m0, m1, g0, g1, keep):
    half, rows = m0.shape
    cols = g0.shape[1]
    tb = tile_blocks(rows // BLK)
    tm = tb * BLK
    return pl.pallas_call(
        functools.partial(out_grad_kernel, tb),
        grid=(rows // tm,),
        out_shape=jax.ShapeDtypeStruct((rows, cols), BF16),
        in_specs=[
            pl.BlockSpec(memory_space=pltpu.SMEM),
            pl.BlockSpec((half, tm), lambda j: (0, j)),
            pl.BlockSpec((half, tm), lambda j: (0, j)),
            pl.BlockSpec((half, cols), lambda j: (0, 0)),
            pl.BlockSpec((half, cols), lambda j: (0, 0)),
        ],
        out_specs=pl.BlockSpec((tm, cols), lambda j: (j, 0)),
        compiler_params=params(),
        cost_estimate=cost(rows, 2 * half, cols, 4 * half * rows + 2 * rows * cols),
    )(keep, m0, m1, g0, g1)


def swap(x, axis, n, bits):
    return lax.ppermute(x, axis, [(i, i ^ bits) for i in range(n)])


def mp_orders(n):
    up = [1 << b for b in range(n.bit_length() - 1)]
    return up, up[::-1]


def scatter_sum(part, n, me):
    rows, cols = part.shape
    levels = n.bit_length() - 1
    piece = rows // (2 * n)
    split = part.reshape(n, 2, piece, cols)
    halves = []
    for half, order in enumerate(mp_orders(n)):
        cur = split[:, half].reshape((2,) * levels + (piece, cols))
        left = list(range(levels))[::-1]
        for stride in order:
            bit = stride.bit_length() - 1
            axis = left.index(bit)
            mine = (me // stride) % 2
            sent = lax.dynamic_index_in_dim(cur, 1 - mine, axis, keepdims=False)
            kept = lax.dynamic_index_in_dim(cur, mine, axis, keepdims=False)
            got = swap(sent.astype(BF16), "mp", n, stride)
            cur = kept.astype(F32) + got.astype(F32)
            left.pop(axis)
        halves.append(cur.reshape(piece, cols))
    return jnp.concatenate(halves, 0)


def gather_tokens(own, n):
    piece = own.shape[0] // 2
    out = []
    for half, order in enumerate(mp_orders(n)):
        pieces = [own[half * piece : (half + 1) * piece]]
        for stride in order:
            pieces += [swap(p, "mp", n, stride) for p in pieces]
        out += pieces
    return jnp.concatenate(out, 0)


def gathered_order(x, n, me):
    piece = x.shape[0] // (2 * n)
    split = x.reshape(n, 2, piece, x.shape[1])
    out = []
    for half, order in enumerate(mp_orders(n)):
        offsets = [0]
        for stride in order:
            offsets += [o ^ stride for o in offsets]
        for o in offsets:
            out.append(lax.dynamic_index_in_dim(split[:, half], me ^ o, 0, keepdims=False))
    return jnp.concatenate(out, 0)


def to_blocks(x):
    return x.reshape(x.shape[0], -1, BLK).transpose(1, 0, 2)


def from_blocks(x):
    return x.transpose(1, 0, 2).reshape(x.shape[1], -1)


def exchange(blocks, picks, back, n, me):
    parts = []
    for s in range(n):
        part = jnp.take(blocks, lax.dynamic_index_in_dim(picks, me ^ s, 0, keepdims=False), axis=0)
        parts.append(part if s == 0 else swap(part, "hidden", n, s))
    return jnp.take(jnp.concatenate(parts, 0), back, axis=0)


def tables(hidden_order, n, me):
    per = hidden_order.shape[0] // n
    cap = -(-per // n)
    ids = hidden_order.reshape(n, per)
    src = ids // per
    k = jnp.arange(per, dtype=jnp.int32)
    same = src[:, :, None] == src[:, None, :]
    rank = jnp.sum(jnp.where(same & (k[None, None, :] < k[None, :, None]), 1, 0), axis=2)
    devs = jnp.arange(n, dtype=jnp.int32)
    slots = jnp.arange(cap, dtype=jnp.int32)
    my_src = lax.dynamic_index_in_dim(src, me, 0, keepdims=False)
    my_rank = lax.dynamic_index_in_dim(rank, me, 0, keepdims=False)
    stored_pick = jnp.sum(
        jnp.where(
            (my_src[None, None, :] == devs[:, None, None])
            & (my_rank[None, None, :] == slots[None, :, None]),
            k[None, None, :],
            0,
        ),
        axis=2,
    )
    hidden_pick = jnp.sum(
        jnp.where(
            (src[:, None, :] == me) & (rank[:, None, :] == slots[None, :, None]),
            (ids - me * per)[:, None, :],
            0,
        ),
        axis=2,
    )
    stored_back = (my_src ^ me) * cap + my_rank
    wanted = me * per + k
    hidden_back = jnp.sum(
        jnp.where(
            ids[None] == wanted[:, None, None],
            ((devs ^ me)[:, None] * cap + rank)[None],
            0,
        ),
        axis=(1, 2),
    )
    return stored_pick, stored_back, hidden_pick, hidden_back


def shards(n_dp, n_mp, n_hidden, tokens, out_grad, gate_weight, up_weight, down_weight, gate_keep, up_keep, down_keep, hidden_order):
    mp = lax.axis_index("mp")
    here = lax.axis_index("hidden")
    stored_pick, stored_back, hidden_pick, hidden_back = tables(hidden_order, n_hidden, here)

    grad_part = times_rows(out_grad, down_weight, down_keep)
    gate_part = times_columns(tokens, gate_weight, gate_keep)
    up_part = times_columns(tokens, up_weight, up_keep)

    grad_stored = scatter_sum(grad_part, n_mp, mp).astype(BF16)
    hidden_grad = from_blocks(
        exchange(to_blocks(grad_stored), stored_pick, hidden_back, n_hidden, here)
    )
    gate = scatter_sum(gate_part, n_mp, mp)
    up = scatter_sum(up_part, n_mp, mp)

    sig = jax.nn.sigmoid(gate)
    act = gate * sig
    hidden_act = (act * up).astype(BF16)
    moved = from_blocks(
        exchange(to_blocks(hidden_act), hidden_pick, stored_back, n_hidden, here)
    )
    hidden_grad = hidden_grad.astype(F32)
    gate_delta = (hidden_grad * up * (sig * (1.0 + gate * (1.0 - sig)))).astype(BF16)
    up_delta = (hidden_grad * act).astype(BF16)

    tok = gathered_order(tokens, n_mp, mp)
    grd = gathered_order(out_grad, n_mp, mp)
    tok_t = jnp.concatenate([tok, swap(tok, "dp", n_dp, 1)], 0).T
    grd_other = swap(grd, "dp", n_dp, 1)

    gate_all = gather_tokens(gate_delta, n_mp)
    gate_grad = in_grad(tok_t, gate_all, swap(gate_all, "dp", n_dp, 1), gate_keep)
    up_all = gather_tokens(up_delta, n_mp)
    up_grad = in_grad(tok_t, up_all, swap(up_all, "dp", n_dp, 1), up_keep)
    moved_all = gather_tokens(moved, n_mp)
    down = down_grad(moved_all, swap(moved_all, "dp", n_dp, 1), grd, grd_other, down_keep)
    return gate_grad, up_grad, down


def solution(mesh):
    placed = (
        P("dp", "mp"),
        P("dp", "mp"),
        P("mp", "hidden"),
        P("mp", "hidden"),
        P("hidden", "mp"),
        P("mp", "hidden"),
        P("mp", "hidden"),
        P("hidden", "mp"),
        P(),
    )
    sizes = (mesh.shape["dp"], mesh.shape["mp"], mesh.shape["hidden"])
    return jax.shard_map(
        functools.partial(shards, *sizes),
        mesh=mesh,
        in_specs=placed,
        out_specs=(P("mp", "hidden"), P("mp", "hidden"), P("hidden", "mp")),
        check_vma=False,
    )
```

```python
import functools

import jax
import jax.numpy as jnp
from jax import lax
from jax.experimental import pallas as pl
from jax.experimental.pallas import tpu as pltpu
from jax.sharding import PartitionSpec as P

BLK = 128
F32 = jnp.float32
BF16 = jnp.bfloat16
NN = (((1,), (0,)), ((), ()))
NT = (((1,), (1,)), ((), ()))
TN = (((0,), (0,)), ((), ()))
VMEM_LIMIT = 48 * 1024 * 1024


def tile_blocks(blocks):
    return max(t for t in (1, 2, 4) if blocks % t == 0)


def params():
    return pltpu.CompilerParams(vmem_limit_bytes=VMEM_LIMIT)


def cost(rows, inner, cols, nbytes):
    return pl.CostEstimate(flops=2 * rows * inner * cols, bytes_accessed=nbytes, transcendentals=0)


def masked_into(dst, src, keep, row0, col0):
    rows, cols = src.shape
    for i in range(rows // BLK):
        for j in range(cols // BLK):
            at = (slice(i * BLK, (i + 1) * BLK), slice(j * BLK, (j + 1) * BLK))
            block = src[at]
            dst[at] = jnp.where(keep[row0 + i, col0 + j] != 0, block, jnp.zeros_like(block))


def columns_kernel(tb, keep, x, w, out, held):
    masked_into(held, w, keep, 0, pl.program_id(0) * tb)
    out[...] = lax.dot_general(x[...], held[...], NN, preferred_element_type=F32).astype(BF16)


def rows_kernel(tb, keep, x, w, out, held):
    masked_into(held, w, keep, pl.program_id(0) * tb, 0)
    out[...] = lax.dot_general(x[...], held[...], NT, preferred_element_type=F32).astype(BF16)


def times_columns(x, w, keep):
    rows, depth = x.shape
    cols = w.shape[1]
    tb = tile_blocks(cols // BLK)
    tn = tb * BLK
    return pl.pallas_call(
        functools.partial(columns_kernel, tb),
        grid=(cols // tn,),
        out_shape=jax.ShapeDtypeStruct((rows, cols), BF16),
        in_specs=[
            pl.BlockSpec(memory_space=pltpu.SMEM),
            pl.BlockSpec((rows, depth), lambda j: (0, 0)),
            pl.BlockSpec((depth, tn), lambda j: (0, j)),
        ],
        out_specs=pl.BlockSpec((rows, tn), lambda j: (0, j)),
        scratch_shapes=[pltpu.VMEM((depth, tn), BF16)],
        compiler_params=params(),
        cost_estimate=cost(rows, depth, cols, 2 * depth * cols + 2 * rows * cols),
    )(keep, x, w)


def times_rows(x, w, keep):
    rows, depth = x.shape
    cols = w.shape[0]
    tb = tile_blocks(cols // BLK)
    tn = tb * BLK
    return pl.pallas_call(
        functools.partial(rows_kernel, tb),
        grid=(cols // tn,),
        out_shape=jax.ShapeDtypeStruct((rows, cols), BF16),
        in_specs=[
            pl.BlockSpec(memory_space=pltpu.SMEM),
            pl.BlockSpec((rows, depth), lambda j: (0, 0)),
            pl.BlockSpec((tn, depth), lambda j: (j, 0)),
        ],
        out_specs=pl.BlockSpec((rows, tn), lambda j: (0, j)),
        scratch_shapes=[pltpu.VMEM((tn, depth), BF16)],
        compiler_params=params(),
        cost_estimate=cost(rows, depth, cols, 2 * depth * cols + 2 * rows * cols),
    )(keep, x, w)


def store_masked(out, value, keep, row0, col0, base):
    rows, cols = value.shape
    for i in range(rows // BLK):
        for j in range(cols // BLK):
            block = value[i * BLK : (i + 1) * BLK, j * BLK : (j + 1) * BLK]
            out[base + i * BLK : base + (i + 1) * BLK, j * BLK : (j + 1) * BLK] = jnp.where(
                keep[row0 + i, col0 + j] != 0, block, jnp.zeros_like(block)
            ).astype(BF16)


def in_grad_kernel(tb, strip, keep, xt, d0, d1, out, both):
    col0 = pl.program_id(0) * tb
    half = d0.shape[0]
    both[:half] = d0[...]
    both[half:] = d1[...]
    for base in range(0, xt.shape[0], strip):
        value = lax.dot_general(
            xt[base : base + strip], both[...], NN, preferred_element_type=F32
        )
        store_masked(out, value, keep, base // BLK, col0, base)


def in_grad(xt, d0, d1, keep):
    rows, depth = xt.shape
    half, cols = d0.shape
    tb = tile_blocks(cols // BLK)
    tn = tb * BLK
    return pl.pallas_call(
        functools.partial(in_grad_kernel, tb, min(512, rows)),
        grid=(cols // tn,),
        out_shape=jax.ShapeDtypeStruct((rows, cols), BF16),
        in_specs=[
            pl.BlockSpec(memory_space=pltpu.SMEM),
            pl.BlockSpec((rows, depth), lambda j: (0, 0)),
            pl.BlockSpec((half, tn), lambda j: (0, j)),
            pl.BlockSpec((half, tn), lambda j: (0, j)),
        ],
        out_specs=pl.BlockSpec((rows, tn), lambda j: (0, j)),
        scratch_shapes=[pltpu.VMEM((2 * half, tn), BF16)],
        compiler_params=params(),
        cost_estimate=cost(rows, depth, cols, 2 * depth * cols + 2 * rows * cols),
    )(keep, xt, d0, d1)


def out_grad_kernel(tb, keep, m0, m1, grads, out, both):
    row0 = pl.program_id(0) * tb
    half = m0.shape[0]
    both[:half] = m0[...]
    both[half:] = m1[...]
    value = lax.dot_general(both[...], grads[...], TN, preferred_element_type=F32)
    store_masked(out, value, keep, row0, 0, 0)


def down_grad(m0, m1, grads, keep):
    half, rows = m0.shape
    cols = grads.shape[1]
    tb = tile_blocks(rows // BLK)
    tm = tb * BLK
    return pl.pallas_call(
        functools.partial(out_grad_kernel, tb),
        grid=(rows // tm,),
        out_shape=jax.ShapeDtypeStruct((rows, cols), BF16),
        in_specs=[
            pl.BlockSpec(memory_space=pltpu.SMEM),
            pl.BlockSpec((half, tm), lambda j: (0, j)),
            pl.BlockSpec((half, tm), lambda j: (0, j)),
            pl.BlockSpec((2 * half, cols), lambda j: (0, 0)),
        ],
        out_specs=pl.BlockSpec((tm, cols), lambda j: (j, 0)),
        scratch_shapes=[pltpu.VMEM((2 * half, tm), BF16)],
        compiler_params=params(),
        cost_estimate=cost(rows, 2 * half, cols, 4 * half * rows + 2 * rows * cols),
    )(keep, m0, m1, grads)


def pick_kernel(idx, x, out):
    for k in range(out.shape[0]):
        out[k] = x[:, pl.ds(pl.multiple_of(idx[k] * BLK, BLK), BLK)]


def pick(x, idx):
    return pl.pallas_call(
        pick_kernel,
        out_shape=jax.ShapeDtypeStruct((idx.shape[0], x.shape[0], BLK), x.dtype),
        in_specs=[
            pl.BlockSpec(memory_space=pltpu.SMEM),
            pl.BlockSpec(memory_space=pltpu.VMEM),
        ],
        out_specs=pl.BlockSpec(memory_space=pltpu.VMEM),
        compiler_params=params(),
        cost_estimate=cost(1, 1, 1, 4 * x.size),
    )(idx, x)


def place_kernel(cap, idx, *refs):
    *parts, out, held = refs
    for p, part in enumerate(parts):
        held[p * cap : (p + 1) * cap] = part[...]
    for k in range(out.shape[1] // BLK):
        out[:, k * BLK : (k + 1) * BLK] = held[idx[k]]


def place(parts, idx):
    cap, rows, _ = parts[0].shape
    return pl.pallas_call(
        functools.partial(place_kernel, cap),
        out_shape=jax.ShapeDtypeStruct((rows, idx.shape[0] * BLK), BF16),
        in_specs=[pl.BlockSpec(memory_space=pltpu.SMEM)]
        + [pl.BlockSpec(memory_space=pltpu.VMEM)] * len(parts),
        out_specs=pl.BlockSpec(memory_space=pltpu.VMEM),
        scratch_shapes=[pltpu.VMEM((cap * len(parts), rows, BLK), BF16)],
        compiler_params=params(),
        cost_estimate=cost(1, 1, 1, 4 * rows * idx.shape[0] * BLK),
    )(idx, *parts)


def swap(x, axis, n, bits):
    return lax.ppermute(x, axis, [(i, i ^ bits) for i in range(n)])


def mp_orders(n):
    up = [1 << b for b in range(n.bit_length() - 1)]
    return up, up[::-1]


def scatter_sum(part, n, me):
    rows, cols = part.shape
    levels = n.bit_length() - 1
    piece = rows // (2 * n)
    dests = (2,) * levels
    split = part.reshape(dests + (2, piece, cols))
    halves = []
    for half, order in enumerate(mp_orders(n)):
        cur = None
        left = list(range(levels))[::-1]
        for stride in order:
            axis = left.index(stride.bit_length() - 1)
            mine = (me // stride) % 2
            if cur is None:
                start = [0] * (levels + 3)
                start[levels] = half
                size = list(dests) + [1, piece, cols]
                size[axis] = 1
                shape = (2,) * (levels - 1) + (piece, cols)
                start[axis] = 1 - mine
                sent = lax.dynamic_slice(split, start, size).reshape(shape)
                start[axis] = mine
                kept = lax.dynamic_slice(split, start, size).reshape(shape)
            else:
                sent = lax.dynamic_index_in_dim(cur, 1 - mine, axis, keepdims=False)
                kept = lax.dynamic_index_in_dim(cur, mine, axis, keepdims=False)
            got = swap(sent.astype(BF16), "mp", n, stride)
            cur = kept.astype(F32) + got.astype(F32)
            left.pop(axis)
        halves.append(cur.reshape(piece, cols))
    return jnp.concatenate(halves, 0)


def gather_pieces(own, n, first=None):
    if n != 4:
        return [own] + [swap(own, "mp", n, s) for s in range(1, n)]
    piece = own.shape[0] // 2
    one = swap(own, "mp", n, 1)
    two = swap(own, "mp", n, 2)
    if first is not None:
        one, two = after(first, (one, two))
    return [own, one, two, swap(one[:piece], "mp", n, 2), swap(two[piece:], "mp", n, 1)]


def gathered_order(x, n, me):
    split = x.reshape(n, x.shape[0] // n, x.shape[1])
    return jnp.concatenate(
        [lax.dynamic_index_in_dim(split, me ^ s, 0, keepdims=False) for s in range(n)], 0
    )


def exchange(x, picks, n):
    cap = picks.shape[0] // n
    blocks = pick(x, picks)
    parts = [blocks[s * cap : (s + 1) * cap] for s in range(n)]
    return [parts[0]] + [swap(parts[s], "hidden", n, s) for s in range(1, n)]


def tables(hidden_order, n, me):
    per = hidden_order.shape[0] // n
    cap = -(-per // n)
    ids = hidden_order.reshape(n, per)
    src = ids // per
    k = jnp.arange(per, dtype=jnp.int32)
    same = src[:, :, None] == src[:, None, :]
    rank = jnp.sum(jnp.where(same & (k[None, None, :] < k[None, :, None]), 1, 0), axis=2)
    devs = jnp.arange(n, dtype=jnp.int32)
    slots = jnp.arange(cap, dtype=jnp.int32)
    my_src = lax.dynamic_index_in_dim(src, me, 0, keepdims=False)
    my_rank = lax.dynamic_index_in_dim(rank, me, 0, keepdims=False)
    stored_back = (my_src ^ me) * cap + my_rank
    places = jnp.arange(n * cap, dtype=jnp.int32)
    stored_pick = jnp.sum(
        jnp.where(stored_back[None, :] == places[:, None], k[None, :], 0), axis=1
    )
    at = (devs ^ me)[:, None] * cap + rank
    wanted = me * per + k
    hidden_back = jnp.sum(
        jnp.where(ids[None] == wanted[:, None, None], at[None], 0), axis=(1, 2)
    )
    hidden_pick = jnp.sum(
        jnp.where((src == me)[None] & (at[None] == places[:, None, None]), (ids - me * per)[None], 0),
        axis=(1, 2),
    )
    return stored_pick, stored_back, hidden_pick, hidden_back


def after(first, value):
    return lax.optimization_barrier((value, first))[0]


def shards(n_dp, n_mp, n_hidden, tokens, out_grad, gate_weight, up_weight, down_weight, gate_keep, up_keep, down_keep, hidden_order):
    mp = lax.axis_index("mp")
    here = lax.axis_index("hidden")

    gate_part = times_columns(tokens, gate_weight, gate_keep)
    up_part = times_columns(tokens, up_weight, after(gate_part, up_keep))
    grad_part = times_rows(out_grad, down_weight, after(up_part, down_keep))
    order = after(gate_part, hidden_order)
    stored_pick, stored_back, hidden_pick, hidden_back = tables(order, n_hidden, here)

    gate = scatter_sum(gate_part, n_mp, mp)
    up = scatter_sum(up_part, n_mp, mp)
    sig = jax.nn.sigmoid(gate)
    act = gate * sig
    hidden_act = (act * up).astype(BF16)
    moved = place(exchange(hidden_act, hidden_pick, n_hidden), stored_back)

    grad_stored = scatter_sum(grad_part, n_mp, mp).astype(BF16)
    arrived = exchange(grad_stored, stored_pick, n_hidden)
    hidden_grad = place(arrived, after(moved, hidden_back)).astype(F32)
    gate_delta = (hidden_grad * up * (sig * (1.0 + gate * (1.0 - sig)))).astype(BF16)
    up_delta = (hidden_grad * act).astype(BF16)

    late_tokens, late_grads = after(grad_part, (tokens, out_grad))
    tok = gathered_order(late_tokens, n_mp, mp)
    grd = gathered_order(late_grads, n_mp, mp)
    grd = jnp.concatenate([grd, swap(grd, "dp", n_dp, 1)], 0)
    tok_t = jnp.concatenate([tok, swap(tok, "dp", n_dp, 1)], 0).T

    moved_all = jnp.concatenate(gather_pieces(moved, n_mp), 0)
    down = down_grad(moved_all, swap(moved_all, "dp", n_dp, 1), grd, down_keep)
    gate_all = jnp.concatenate(gather_pieces(gate_delta, n_mp), 0)
    gate_other = after(down, swap(gate_all, "dp", n_dp, 1))
    gate_grad = in_grad(tok_t, gate_all, gate_other, gate_keep)
    up_all = jnp.concatenate(gather_pieces(up_delta, n_mp, down), 0)
    up_other = after(gate_grad, swap(up_all, "dp", n_dp, 1))
    up_grad = in_grad(tok_t, up_all, up_other, up_keep)
    return gate_grad, up_grad, down


def solution(mesh):
    placed = (
        P("dp", "mp"),
        P("dp", "mp"),
        P("mp", "hidden"),
        P("mp", "hidden"),
        P("hidden", "mp"),
        P("mp", "hidden"),
        P("mp", "hidden"),
        P("hidden", "mp"),
        P(),
    )
    sizes = (mesh.shape["dp"], mesh.shape["mp"], mesh.shape["hidden"])
    return jax.shard_map(
        functools.partial(shards, *sizes),
        mesh=mesh,
        in_specs=placed,
        out_specs=(P("mp", "hidden"), P("mp", "hidden"), P("hidden", "mp")),
        check_vma=False,
    )
```

```python
import functools

import jax
import jax.numpy as jnp
from jax import lax
from jax.experimental import pallas as pl
from jax.experimental.pallas import tpu as pltpu
from jax.sharding import PartitionSpec as P

BLK = 128
F32 = jnp.float32
BF16 = jnp.bfloat16
NN = (((1,), (0,)), ((), ()))
NT = (((1,), (1,)), ((), ()))
TN = (((0,), (0,)), ((), ()))
VMEM_LIMIT = 48 * 1024 * 1024


def tile_blocks(blocks):
    return max(t for t in (1, 2, 4) if blocks % t == 0)


def params():
    return pltpu.CompilerParams(vmem_limit_bytes=VMEM_LIMIT)


def cost(rows, inner, cols, nbytes):
    return pl.CostEstimate(flops=2 * rows * inner * cols, bytes_accessed=nbytes, transcendentals=0)


def masked_into(dst, src, keep, row0, col0):
    rows, cols = src.shape
    for i in range(rows // BLK):
        for j in range(cols // BLK):
            at = (slice(i * BLK, (i + 1) * BLK), slice(j * BLK, (j + 1) * BLK))
            block = src[at]
            dst[at] = jnp.where(keep[row0 + i, col0 + j] != 0, block, jnp.zeros_like(block))


def columns_kernel(tb, keep, x, w, out, held):
    masked_into(held, w, keep, 0, pl.program_id(0) * tb)
    out[...] = lax.dot_general(x[...], held[...], NN, preferred_element_type=F32).astype(BF16)


def rows_kernel(tb, keep, x, w, out, held):
    masked_into(held, w, keep, pl.program_id(0) * tb, 0)
    out[...] = lax.dot_general(x[...], held[...], NT, preferred_element_type=F32).astype(BF16)


def times_columns(x, w, keep):
    rows, depth = x.shape
    cols = w.shape[1]
    tb = tile_blocks(cols // BLK)
    tn = tb * BLK
    return pl.pallas_call(
        functools.partial(columns_kernel, tb),
        grid=(cols // tn,),
        out_shape=jax.ShapeDtypeStruct((rows, cols), BF16),
        in_specs=[
            pl.BlockSpec(memory_space=pltpu.SMEM),
            pl.BlockSpec((rows, depth), lambda j: (0, 0)),
            pl.BlockSpec((depth, tn), lambda j: (0, j)),
        ],
        out_specs=pl.BlockSpec((rows, tn), lambda j: (0, j)),
        scratch_shapes=[pltpu.VMEM((depth, tn), BF16)],
        compiler_params=params(),
        cost_estimate=cost(rows, depth, cols, 2 * depth * cols + 2 * rows * cols),
    )(keep, x, w)


def times_rows(x, w, keep):
    rows, depth = x.shape
    cols = w.shape[0]
    tb = tile_blocks(cols // BLK)
    tn = tb * BLK
    return pl.pallas_call(
        functools.partial(rows_kernel, tb),
        grid=(cols // tn,),
        out_shape=jax.ShapeDtypeStruct((rows, cols), BF16),
        in_specs=[
            pl.BlockSpec(memory_space=pltpu.SMEM),
            pl.BlockSpec((rows, depth), lambda j: (0, 0)),
            pl.BlockSpec((tn, depth), lambda j: (j, 0)),
        ],
        out_specs=pl.BlockSpec((rows, tn), lambda j: (0, j)),
        scratch_shapes=[pltpu.VMEM((tn, depth), BF16)],
        compiler_params=params(),
        cost_estimate=cost(rows, depth, cols, 2 * depth * cols + 2 * rows * cols),
    )(keep, x, w)


def store_masked(out, value, keep, row0, col0, base):
    rows, cols = value.shape
    for i in range(rows // BLK):
        for j in range(cols // BLK):
            block = value[i * BLK : (i + 1) * BLK, j * BLK : (j + 1) * BLK]
            out[base + i * BLK : base + (i + 1) * BLK, j * BLK : (j + 1) * BLK] = jnp.where(
                keep[row0 + i, col0 + j] != 0, block, jnp.zeros_like(block)
            ).astype(BF16)


def stack(both, pieces):
    at = 0
    for piece in pieces:
        both[at : at + piece.shape[0]] = piece[...]
        at += piece.shape[0]


def in_grad_kernel(tb, strip, keep, xt, *refs):
    *pieces, out, both = refs
    col0 = pl.program_id(0) * tb
    stack(both, pieces)
    for base in range(0, xt.shape[0], strip):
        value = lax.dot_general(
            xt[base : base + strip], both[...], NN, preferred_element_type=F32
        )
        store_masked(out, value, keep, base // BLK, col0, base)


def in_grad(xt, pieces, keep):
    rows, depth = xt.shape
    cols = pieces[0].shape[1]
    tb = tile_blocks(cols // BLK)
    tn = tb * BLK
    return pl.pallas_call(
        functools.partial(in_grad_kernel, tb, min(512, rows)),
        grid=(cols // tn,),
        out_shape=jax.ShapeDtypeStruct((rows, cols), BF16),
        in_specs=[
            pl.BlockSpec(memory_space=pltpu.SMEM),
            pl.BlockSpec((rows, depth), lambda j: (0, 0)),
        ]
        + [pl.BlockSpec((p.shape[0], tn), lambda j: (0, j)) for p in pieces],
        out_specs=pl.BlockSpec((rows, tn), lambda j: (0, j)),
        scratch_shapes=[pltpu.VMEM((depth, tn), BF16)],
        compiler_params=params(),
        cost_estimate=cost(rows, depth, cols, 2 * depth * cols + 2 * rows * cols),
    )(keep, xt, *pieces)


def out_grad_kernel(tb, keep, grads, *refs):
    *pieces, out, both = refs
    row0 = pl.program_id(0) * tb
    stack(both, pieces)
    value = lax.dot_general(both[...], grads[...], TN, preferred_element_type=F32)
    store_masked(out, value, keep, row0, 0, 0)


def down_grad(pieces, grads, keep):
    rows = pieces[0].shape[1]
    depth, cols = grads.shape
    tb = tile_blocks(rows // BLK)
    tm = tb * BLK
    return pl.pallas_call(
        functools.partial(out_grad_kernel, tb),
        grid=(rows // tm,),
        out_shape=jax.ShapeDtypeStruct((rows, cols), BF16),
        in_specs=[
            pl.BlockSpec(memory_space=pltpu.SMEM),
            pl.BlockSpec((depth, cols), lambda j: (0, 0)),
        ]
        + [pl.BlockSpec((p.shape[0], tm), lambda j: (0, j)) for p in pieces],
        out_specs=pl.BlockSpec((tm, cols), lambda j: (j, 0)),
        scratch_shapes=[pltpu.VMEM((depth, tm), BF16)],
        compiler_params=params(),
        cost_estimate=cost(rows, depth, cols, 2 * depth * rows + 2 * rows * cols),
    )(keep, grads, *pieces)


def pick_kernel(idx, x, out):
    for k in range(out.shape[0]):
        out[k] = x[:, pl.ds(pl.multiple_of(idx[k] * BLK, BLK), BLK)]


def pick(x, idx):
    return pl.pallas_call(
        pick_kernel,
        out_shape=jax.ShapeDtypeStruct((idx.shape[0], x.shape[0], BLK), x.dtype),
        in_specs=[
            pl.BlockSpec(memory_space=pltpu.SMEM),
            pl.BlockSpec(memory_space=pltpu.VMEM),
        ],
        out_specs=pl.BlockSpec(memory_space=pltpu.VMEM),
        compiler_params=params(),
        cost_estimate=cost(1, 1, 1, 4 * x.size),
    )(idx, x)


def place_kernel(cap, idx, *refs):
    *parts, out, held = refs
    for p, part in enumerate(parts):
        held[p * cap : (p + 1) * cap] = part[...]
    for k in range(out.shape[1] // BLK):
        out[:, k * BLK : (k + 1) * BLK] = held[idx[k]]


def place(parts, idx):
    cap, rows, _ = parts[0].shape
    return pl.pallas_call(
        functools.partial(place_kernel, cap),
        out_shape=jax.ShapeDtypeStruct((rows, idx.shape[0] * BLK), BF16),
        in_specs=[pl.BlockSpec(memory_space=pltpu.SMEM)]
        + [pl.BlockSpec(memory_space=pltpu.VMEM)] * len(parts),
        out_specs=pl.BlockSpec(memory_space=pltpu.VMEM),
        scratch_shapes=[pltpu.VMEM((cap * len(parts), rows, BLK), BF16)],
        compiler_params=params(),
        cost_estimate=cost(1, 1, 1, 4 * rows * idx.shape[0] * BLK),
    )(idx, *parts)


def swap(x, axis, n, bits):
    return lax.ppermute(x, axis, [(i, i ^ bits) for i in range(n)])


def mp_orders(n):
    up = [1 << b for b in range(n.bit_length() - 1)]
    return up, up[::-1]


def scatter_sum(part, n, me):
    rows, cols = part.shape
    levels = n.bit_length() - 1
    piece = rows // (2 * n)
    dests = (2,) * levels
    split = part.reshape(dests + (2, piece, cols))
    halves = []
    for half, order in enumerate(mp_orders(n)):
        cur = None
        left = list(range(levels))[::-1]
        for stride in order:
            axis = left.index(stride.bit_length() - 1)
            mine = (me // stride) % 2
            if cur is None:
                start = [0] * (levels + 3)
                start[levels] = half
                size = list(dests) + [1, piece, cols]
                size[axis] = 1
                shape = (2,) * (levels - 1) + (piece, cols)
                start[axis] = 1 - mine
                sent = lax.dynamic_slice(split, start, size).reshape(shape)
                start[axis] = mine
                kept = lax.dynamic_slice(split, start, size).reshape(shape)
            else:
                sent = lax.dynamic_index_in_dim(cur, 1 - mine, axis, keepdims=False)
                kept = lax.dynamic_index_in_dim(cur, mine, axis, keepdims=False)
            got = swap(sent.astype(BF16), "mp", n, stride)
            cur = kept.astype(F32) + got.astype(F32)
            left.pop(axis)
        halves.append(cur.reshape(piece, cols))
    return jnp.concatenate(halves, 0)


def gather_pieces(own, n, first=None):
    if n != 4:
        return [own] + [swap(own, "mp", n, s) for s in range(1, n)]
    piece = own.shape[0] // 2
    one = swap(own, "mp", n, 1)
    two = swap(own, "mp", n, 2)
    if first is not None:
        one, two = after(first, (one, two))
    return [own, one, two, swap(one[:piece], "mp", n, 2), swap(two[piece:], "mp", n, 1)]


def both_groups(pieces, n_dp):
    early, late = pieces[:3], pieces[3:]
    other = [swap(jnp.concatenate(part, 0), "dp", n_dp, 1) for part in (early, late) if part]
    return pieces + other


def gathered_order(x, n, me):
    split = x.reshape(n, x.shape[0] // n, x.shape[1])
    return jnp.concatenate(
        [lax.dynamic_index_in_dim(split, me ^ s, 0, keepdims=False) for s in range(n)], 0
    )


def exchange(x, picks, n):
    cap = picks.shape[0] // n
    blocks = pick(x, picks)
    parts = [blocks[s * cap : (s + 1) * cap] for s in range(n)]
    return [parts[0]] + [swap(parts[s], "hidden", n, s) for s in range(1, n)]


def tables(hidden_order, n, me):
    per = hidden_order.shape[0] // n
    cap = -(-per // n)
    ids = hidden_order.reshape(n, per)
    src = ids // per
    k = jnp.arange(per, dtype=jnp.int32)
    same = src[:, :, None] == src[:, None, :]
    rank = jnp.sum(jnp.where(same & (k[None, None, :] < k[None, :, None]), 1, 0), axis=2)
    devs = jnp.arange(n, dtype=jnp.int32)
    slots = jnp.arange(cap, dtype=jnp.int32)
    my_src = lax.dynamic_index_in_dim(src, me, 0, keepdims=False)
    my_rank = lax.dynamic_index_in_dim(rank, me, 0, keepdims=False)
    stored_back = (my_src ^ me) * cap + my_rank
    places = jnp.arange(n * cap, dtype=jnp.int32)
    stored_pick = jnp.sum(
        jnp.where(stored_back[None, :] == places[:, None], k[None, :], 0), axis=1
    )
    at = (devs ^ me)[:, None] * cap + rank
    wanted = me * per + k
    hidden_back = jnp.sum(
        jnp.where(ids[None] == wanted[:, None, None], at[None], 0), axis=(1, 2)
    )
    hidden_pick = jnp.sum(
        jnp.where((src == me)[None] & (at[None] == places[:, None, None]), (ids - me * per)[None], 0),
        axis=(1, 2),
    )
    return stored_pick, stored_back, hidden_pick, hidden_back


def after(first, value):
    return lax.optimization_barrier((value, first))[0]


def shards(n_dp, n_mp, n_hidden, tokens, out_grad, gate_weight, up_weight, down_weight, gate_keep, up_keep, down_keep, hidden_order):
    mp = lax.axis_index("mp")
    here = lax.axis_index("hidden")

    gate_part = times_columns(tokens, gate_weight, gate_keep)
    up_part = times_columns(tokens, up_weight, after(gate_part, up_keep))
    grad_part = times_rows(out_grad, down_weight, after(up_part, down_keep))
    order = after(gate_part, hidden_order)
    stored_pick, stored_back, hidden_pick, hidden_back = tables(order, n_hidden, here)

    gate = scatter_sum(gate_part, n_mp, mp)
    up = scatter_sum(up_part, n_mp, mp)
    sig = jax.nn.sigmoid(gate)
    act = gate * sig
    hidden_act = (act * up).astype(BF16)
    moved = place(exchange(hidden_act, hidden_pick, n_hidden), stored_back)

    grad_stored = scatter_sum(grad_part, n_mp, mp).astype(BF16)
    arrived = exchange(grad_stored, stored_pick, n_hidden)
    hidden_grad = place(arrived, after(moved, hidden_back)).astype(F32)
    gate_delta = (hidden_grad * up * (sig * (1.0 + gate * (1.0 - sig)))).astype(BF16)
    up_delta = (hidden_grad * act).astype(BF16)

    late_tokens, late_grads = after(grad_part, (tokens, out_grad))
    tok = gathered_order(late_tokens, n_mp, mp)
    grd = gathered_order(late_grads, n_mp, mp)
    grd = jnp.concatenate([grd, swap(grd, "dp", n_dp, 1)], 0)
    tok_t = jnp.concatenate([tok, swap(tok, "dp", n_dp, 1)], 0).T

    down = down_grad(both_groups(gather_pieces(moved, n_mp), n_dp), grd, down_keep)
    gate_pieces = gather_pieces(gate_delta, n_mp)
    gate_pieces[3:] = after(down, gate_pieces[3:])
    gate_grad = in_grad(tok_t, both_groups(gate_pieces, n_dp), gate_keep)
    up_pieces = gather_pieces(up_delta, n_mp, down)
    up_pieces[3:] = after(gate_grad, up_pieces[3:])
    up_grad = in_grad(tok_t, both_groups(up_pieces, n_dp), up_keep)
    return gate_grad, up_grad, down


def solution(mesh):
    placed = (
        P("dp", "mp"),
        P("dp", "mp"),
        P("mp", "hidden"),
        P("mp", "hidden"),
        P("hidden", "mp"),
        P("mp", "hidden"),
        P("mp", "hidden"),
        P("hidden", "mp"),
        P(),
    )
    sizes = (mesh.shape["dp"], mesh.shape["mp"], mesh.shape["hidden"])
    return jax.shard_map(
        functools.partial(shards, *sizes),
        mesh=mesh,
        in_specs=placed,
        out_specs=(P("mp", "hidden"), P("mp", "hidden"), P("hidden", "mp")),
        check_vma=False,
    )
```
